256 devices in a mesh: section: 16 (over y, z_hi, core), expert: 16 (over x, z_lo).
Axes of the slice: x: 4, y: 4, z: 8 (z_hi: 2, z_lo: 4; z = z_hi * 4 + z_lo), core: 2. Of those that a mesh axis runs over, the one named last changes fastest.
Arguments:
- fwd_tokens: bfloat16 [16, 512, 4096], P('section', 'expert'), may hold values from -6 to 6
- bwd_tokens: bfloat16 [16, 512, 4096], P('section', 'expert'), may hold values from -6 to 6
- out_grads: bfloat16 [16, 512, 4096], P('section', 'expert'), may hold values from -6 to 6
- w_gate: bfloat16 [16, 3072, 4096], P('section', 'expert'), may hold values from -0.09375 to 0.09375
- w_up: bfloat16 [16, 3072, 4096], P('section', 'expert'), may hold values from -0.09375 to 0.09375
- w_down: bfloat16 [16, 3072, 4096], P('section', 'expert'), may hold values from -0.15625 to 0.15625
- fwd_blocks: int32 [16, 2, 3], P('section'), may hold values from -1 to 3, as said below
- bwd_blocks: int32 [16, 2, 3], P('section'), may hold values from -1 to 3, as said below
- fwd_buckets: int32 [16, 512, 2], P('section', 'expert'), may hold values from 0 to 15
- bwd_buckets: int32 [16, 512, 2], P('section', 'expert'), may hold values from 0 to 15
Outputs:
- to_next: bfloat16 [16, 512, 4096], P('section', 'expert')
- to_prev: bfloat16 [16, 512, 4096], P('section', 'expert')
- grad_gate: bfloat16 [16, 3072, 4096], P('section', 'expert')
- grad_up: bfloat16 [16, 3072, 4096], P('section', 'expert')
- grad_down: bfloat16 [16, 3072, 4096], P('section', 'expert')
The draws below stay inside these ranges and needn't reach their ends.
Inputs may be any that keep to these rules, and one draw needn't show every extreme that they name: `fwd_blocks`: for each section and expert the first entries are distinct block numbers in increasing order and the remaining entries are -1; every expert lists at least one block, and in every section some expert lists 3 blocks. `bwd_blocks`: as for fwd_blocks.
All inputs are finite; a program needn't handle non-finite values.
Results may differ from the reference program's by a relative error of at most 0.017.
Values may be sent and summed in bfloat16 or wider, within the bound.
No kernel may reach another device: no remote copies, remote signals or barrier semaphores. Data moves between devices by JAX's collectives and lax.ppermute only.
A program may use at most 128 MiB of HBM per device.

```python
import jax
import jax.numpy as jnp
from jax import lax

D = 4096
FF = 1536
BLOCK = 128
HSPLIT = 8
NBUCKET = 16
TOKENS = 512
NBLK = 4
MAXB = 3
EXP_GRP = 2
N_SECTION = 16


def select_blocks(key):
    first, second, third = jax.random.split(key, 3)
    places = jnp.arange(NBLK, dtype=jnp.int32)
    scores = jax.random.randint(first, (N_SECTION, EXP_GRP, NBLK), 0, 1 << 20) * NBLK + places
    order = jnp.argsort(scores, axis=-1)
    ranks = jnp.argsort(order, axis=-1)
    amount = jax.random.randint(second, (N_SECTION, EXP_GRP), 1, MAXB + 1)
    fullest = jax.random.randint(third, (N_SECTION,), 0, EXP_GRP)
    amount = jnp.where(jnp.arange(EXP_GRP)[None, :] == fullest[:, None], MAXB, amount)
    keep = ranks < amount[:, :, None]
    ordered = jnp.sort(jnp.where(keep, places, NBLK + places), axis=-1)[:, :, :MAXB]
    return jnp.where(ordered < NBLK, ordered, -1).astype(jnp.int32)


def draw_fwd_blocks(key, part):
    key = jax.random.fold_in(key, 11)
    return select_blocks(key)


def draw_bwd_blocks(key, part):
    key = jax.random.fold_in(key, 23)
    return select_blocks(key)


def set_ends(values, rng, least, largest):
    place = [jax.random.randint(jax.random.fold_in(rng, axis), (), 0, length) for axis, length in enumerate(values.shape)]
    main_axis = values.shape.index(max(values.shape))
    beside = place[:main_axis] + [(place[main_axis] + 1) % values.shape[main_axis]] + place[main_axis + 1:]
    return values.at[tuple(place)].set(least).at[tuple(beside)].set(largest)


def block_scale(own_key, extent, shards, low, top_value):
    gain = 1.0
    for dim, shards_of in shards:
        steps = jax.random.uniform(jax.random.fold_in(jax.random.fold_in(own_key, 6), dim), (shards_of,), jnp.float32, low / len(shards), top_value / len(shards))
        gain = gain * jnp.repeat(jnp.exp(steps), extent[dim] // shards_of).reshape((-1,) + (1,) * (len(extent) - 1 - dim))
    return gain


def gaussian(rng, extent, scale, limit, pieces=(), kind=jnp.bfloat16):
    result = jax.random.normal(rng, extent, jnp.float32) * scale
    if len(pieces) > 0:
        result = block_scale(rng, extent, pieces, -0.22, 0.18) * result
    return jnp.clip(result, min=-limit, max=limit).astype(kind)


def setup_inputs(seed: int = 0) -> dict:
    key_of = jax.random.split(jax.random.key(seed), 11)
    fwd_tokens = gaussian(key_of[0], (N_SECTION, TOKENS, D), 1.0, 6.0, ((0, 16), (1, 16)))
    bwd_tokens = gaussian(key_of[1], (N_SECTION, TOKENS, D), 1.0, 6.0, ((0, 16), (1, 16)))
    out_grads = gaussian(key_of[2], (N_SECTION, TOKENS, D), 1.0, 6.0, ((0, 16), (1, 16)))
    w_gate = gaussian(key_of[3], (N_SECTION, EXP_GRP * FF, D), D ** -0.5, 0.09375, ((0, 16), (1, 16)))
    w_up = gaussian(key_of[4], (N_SECTION, EXP_GRP * FF, D), D ** -0.5, 0.09375, ((0, 16), (1, 16)))
    w_down = gaussian(key_of[5], (N_SECTION, EXP_GRP * FF, D), FF ** -0.5, 0.15625, ((0, 16), (1, 16)))
    fwd_blocks = draw_fwd_blocks(jax.random.fold_in(key_of[10], 71), 0)
    bwd_blocks = draw_bwd_blocks(jax.random.fold_in(key_of[10], 71), 0)
    fwd_buckets = set_ends(jax.random.randint(key_of[8], (N_SECTION, TOKENS, EXP_GRP), 0, NBUCKET), jax.random.fold_in(key_of[8], 1), 0, NBUCKET - 1).astype(jnp.int32)
    bwd_buckets = set_ends(jax.random.randint(key_of[9], (N_SECTION, TOKENS, EXP_GRP), 0, NBUCKET), jax.random.fold_in(key_of[9], 1), 0, NBUCKET - 1).astype(jnp.int32)
    return {"fwd_tokens": fwd_tokens, "bwd_tokens": bwd_tokens, "out_grads": out_grads, "w_gate": w_gate, "w_up": w_up, "w_down": w_down, "fwd_blocks": fwd_blocks, "bwd_blocks": bwd_blocks, "fwd_buckets": fwd_buckets, "bwd_buckets": bwd_buckets}


def rank_gate(ids):
    onehot = (ids[:, :, None] == jnp.arange(NBUCKET, dtype=jnp.int32)[None, None, :]).astype(jnp.float32)
    counts = jnp.sum(onehot, axis=0)
    cumul = jnp.cumsum(counts, axis=-1)
    below = jnp.sum(onehot * cumul[None], axis=-1)
    return ((1.0 + below) / (1.0 + TOKENS)).astype(jnp.bfloat16)


def rounded_term(term):
    narrow = lax.optimization_barrier(term.astype(jnp.bfloat16))
    return narrow.astype(jnp.float32)


def one_section(item):
    fwd_x, bwd_x, cotan, gate_w, up_w, down_w, blocks_f, blocks_b, marks_f, marks_b = item
    gates_f = rank_gate(marks_f)
    gates_b = rank_gate(marks_b)
    width = FF // HSPLIT
    moe_total = jnp.zeros((TOKENS, D), jnp.float32)
    back_total = jnp.zeros((TOKENS, D), jnp.float32)
    grads_gate = []
    grads_up = []
    grads_down = []
    for expert in range(EXP_GRP):
        for piece in range(HSPLIT):
            first = expert * FF + piece * width
            w_g = gate_w[first:first + width]
            w_u = up_w[first:first + width]
            w_d = down_w[first:first + width]
            partial_value = jnp.zeros((TOKENS, D), jnp.float32)
            back = jnp.zeros((TOKENS, D), jnp.float32)
            acc_g = jnp.zeros((width, D), jnp.float32)
            acc_u = jnp.zeros((width, D), jnp.float32)
            acc_d = jnp.zeros((width, D), jnp.float32)
            for slot in range(MAXB):
                block = blocks_f[expert, slot]
                valid = (block >= 0).astype(jnp.float32)
                start = (jnp.maximum(block, 0) * BLOCK).astype(jnp.int32)
                rows = lax.dynamic_slice_in_dim(fwd_x, start, BLOCK, 0)
                weight = lax.dynamic_slice_in_dim(gates_f[:, expert], start, BLOCK, 0).astype(jnp.float32) * valid
                pre_gate = jnp.dot(rows, w_g.T, preferred_element_type=jnp.float32)
                pre_up = jnp.dot(rows, w_u.T, preferred_element_type=jnp.float32)
                hidden = (pre_gate * jax.nn.sigmoid(pre_gate) * pre_up).astype(jnp.bfloat16)
                output = jnp.dot(hidden, w_d, preferred_element_type=jnp.float32)
                current = lax.dynamic_slice_in_dim(partial_value, start, BLOCK, 0)
                partial_value = lax.dynamic_update_slice_in_dim(partial_value, current + weight[:, None] * output, start, 0)

                block = blocks_b[expert, slot]
                valid = (block >= 0).astype(jnp.float32)
                start = (jnp.maximum(block, 0) * BLOCK).astype(jnp.int32)
                rows = lax.dynamic_slice_in_dim(bwd_x, start, BLOCK, 0)
                grads_in = lax.dynamic_slice_in_dim(cotan, start, BLOCK, 0)
                weight = lax.dynamic_slice_in_dim(gates_b[:, expert], start, BLOCK, 0).astype(jnp.float32) * valid
                scaled = (weight[:, None] * grads_in.astype(jnp.float32)).astype(jnp.bfloat16)
                d_hidden = jnp.dot(scaled, w_d.T, preferred_element_type=jnp.float32)
                b_gate = jnp.dot(rows, w_g.T, preferred_element_type=jnp.float32)
                b_up = jnp.dot(rows, w_u.T, preferred_element_type=jnp.float32)
                sig = jax.nn.sigmoid(b_gate)
                active = b_gate * sig
                d_gate = (d_hidden * b_up * sig * (1.0 + b_gate * (1.0 - sig))).astype(jnp.bfloat16)
                d_up = (d_hidden * active).astype(jnp.bfloat16)
                b_hidden = (active * b_up).astype(jnp.bfloat16)
                d_rows = jnp.dot(d_gate, w_g, preferred_element_type=jnp.float32) + jnp.dot(d_up, w_u, preferred_element_type=jnp.float32)
                current = lax.dynamic_slice_in_dim(back, start, BLOCK, 0)
                back = lax.dynamic_update_slice_in_dim(back, current + d_rows, start, 0)
                acc_g = acc_g + jnp.dot(d_gate.T, rows, preferred_element_type=jnp.float32)
                acc_u = acc_u + jnp.dot(d_up.T, rows, preferred_element_type=jnp.float32)
                acc_d = acc_d + jnp.dot(b_hidden.T, scaled, preferred_element_type=jnp.float32)
            moe_total = moe_total + rounded_term(partial_value)
            back_total = back_total + rounded_term(back)
            grads_gate.append(acc_g.astype(jnp.bfloat16))
            grads_up.append(acc_u.astype(jnp.bfloat16))
            grads_down.append(acc_d.astype(jnp.bfloat16))
    out_f = (fwd_x.astype(jnp.float32) + moe_total).astype(jnp.bfloat16)
    d_in = (cotan.astype(jnp.float32) + back_total).astype(jnp.bfloat16)
    return (out_f, d_in, jnp.concatenate(grads_gate, axis=0), jnp.concatenate(grads_up, axis=0), jnp.concatenate(grads_down, axis=0))


def reference(fwd_tokens, bwd_tokens, out_grads, w_gate, w_up, w_down, fwd_blocks, bwd_blocks, fwd_buckets, bwd_buckets):
    out_f, d_in, grad_gate, grad_up, grad_down = lax.map(one_section, (fwd_tokens, bwd_tokens, out_grads, w_gate, w_up, w_down, fwd_blocks, bwd_blocks, fwd_buckets, bwd_buckets))
    to_next = jnp.concatenate([jnp.zeros_like(out_f[:1]), out_f[:-1]], axis=0)
    to_prev = jnp.concatenate([d_in[1:], jnp.zeros_like(d_in[:1])], axis=0)
    return (to_next, to_prev, grad_gate, grad_up, grad_down)
```

```python
import jax
import jax.numpy as jnp
from jax import lax
from jax.sharding import PartitionSpec as P

BLOCK = 128
HSPLIT = 8
NX = 4
NZ = 4


def shift_x(a, by):
    pairs = [(x * NZ + z, (x + by) % NX * NZ + z) for x in range(NX) for z in range(NZ)]
    return lax.ppermute(a, "expert", pairs)


def shift_z(a, by):
    pairs = [(x * NZ + z, x * NZ + (z + by) % NZ) for x in range(NX) for z in range(NZ)]
    return lax.ppermute(a, "expert", pairs)


def from_behind(x, axis, by):
    length = lax.axis_size(axis)
    pairs = [(i, i + by) for i in range(length) if 0 <= i + by < length]
    return lax.ppermute(x, axis, pairs)


def gather_small(own):
    line = jnp.stack([own] + [shift_z(own, k) for k in range(1, NZ)])
    return jnp.concatenate([line] + [shift_x(line, k) for k in range(1, NX)], axis=0)


def gather(own):
    chunks = [own] + [shift_z(own, k) for k in range(1, NZ)]
    low = jnp.concatenate(chunks[:2], axis=0)
    high = jnp.concatenate(chunks[2:], axis=0)
    low_1 = shift_x(low, 1)
    high_3 = shift_x(high, -1)
    high_1 = shift_x(high, 1)
    low_3 = shift_x(low, -1)
    low_2 = shift_x(low_1, 1)
    high_2 = shift_x(high_3, -1)
    return jnp.concatenate([low, high, low_1, high_1, low_2, high_2, low_3, high_3], axis=0)


def added(*terms):
    total = terms[0].astype(jnp.float32)
    for term in terms[1:]:
        total = total + term.astype(jnp.float32)
    return total


def scatter(parts):
    half = BLOCK // 2
    low_0, high_0, low_1, high_1, low_2, high_2, low_3, high_3 = [
        parts[i * half:(i + 1) * half] for i in range(8)
    ]
    low_2 = shift_x(low_2, -1)
    high_2 = shift_x(high_2, 1)
    high_1 = shift_x(high_1, -1)
    low_3 = shift_x(low_3, 1)
    low_1 = shift_x(added(low_1, low_2).astype(jnp.bfloat16), -1)
    high_3 = shift_x(added(high_3, high_2).astype(jnp.bfloat16), 1)
    low = added(low_0, low_1, low_3)
    high = added(high_0, high_1, high_3)
    rows = BLOCK // NZ
    back_1 = shift_z(low[rows:].astype(jnp.bfloat16), -1)
    back_2 = shift_z(high[:rows].astype(jnp.bfloat16), -2)
    back_3 = shift_z(high[rows:].astype(jnp.bfloat16), -3)
    return added(low[:rows], back_1, back_2, back_3)


def weights_of(marks, valid, total):
    below = jnp.sum((marks[None, :] <= marks[:, None]).astype(jnp.float32), axis=1)
    gates = ((1.0 + below) / (1.0 + total)).astype(jnp.bfloat16)
    return gates.astype(jnp.float32) * jnp.repeat(valid, BLOCK)


def chosen(blocks, x):
    order = lax.rem(x - jnp.arange(NX, dtype=jnp.int32) + NX, NX)
    return jnp.any(blocks[None, :] == order[:, None], axis=1).astype(jnp.float32)


def across(a, b):
    return lax.dot_general(a, b, (((1,), (1,)), ((), ())), preferred_element_type=jnp.float32)


def onto(a, b):
    return lax.dot_general(a, b, (((0,), (0,)), ((), ())), preferred_element_type=jnp.float32)


def local(
    fwd_tokens,
    bwd_tokens,
    out_grads,
    w_gate,
    w_up,
    w_down,
    fwd_blocks,
    bwd_blocks,
    fwd_buckets,
    bwd_buckets,
):
    place = lax.axis_index("expert")
    group = place // HSPLIT
    x = place // NZ
    total = fwd_tokens.shape[1] * lax.axis_size("expert")
    fwd_x = fwd_tokens[0]
    bwd_x = bwd_tokens[0]
    cotan = out_grads[0]
    gate_w = w_gate[0]
    up_w = w_up[0]
    down_w = w_down[0]
    marks = gather_small(jnp.stack([fwd_buckets[0].T, bwd_buckets[0].T]))
    marks = lax.dynamic_index_in_dim(marks, group, 2, keepdims=False)
    valid_f = chosen(lax.dynamic_index_in_dim(fwd_blocks[0], group, 0, keepdims=False), x)
    valid_b = chosen(lax.dynamic_index_in_dim(bwd_blocks[0], group, 0, keepdims=False), x)
    column_f = weights_of(marks[:, 0].reshape(total), valid_f, total)
    column_b = weights_of(marks[:, 1].reshape(total), valid_b, total)

    rows_b = gather(bwd_x)
    rows_dy = gather(cotan)
    rows_f = gather(fwd_x)

    b_gate = across(rows_b, gate_w)
    b_up = across(rows_b, up_w)
    scaled = (column_b[:, None] * rows_dy.astype(jnp.float32)).astype(jnp.bfloat16)
    d_hidden = across(scaled, down_w)
    sig = jax.nn.sigmoid(b_gate)
    active = b_gate * sig
    d_gate = (d_hidden * b_up * sig * (1.0 + b_gate * (1.0 - sig))).astype(jnp.bfloat16)
    d_up = (d_hidden * active).astype(jnp.bfloat16)
    b_hidden = (active * b_up).astype(jnp.bfloat16)
    back = jnp.dot(d_gate, gate_w, preferred_element_type=jnp.float32) + jnp.dot(
        d_up, up_w, preferred_element_type=jnp.float32
    )
    bwd_total = scatter(back.astype(jnp.bfloat16))
    d_in = (cotan.astype(jnp.float32) + bwd_total).astype(jnp.bfloat16)
    sent_prev = from_behind(d_in, "section", -1)

    pre_gate = across(rows_f, gate_w)
    pre_up = across(rows_f, up_w)
    hidden = (pre_gate * jax.nn.sigmoid(pre_gate) * pre_up).astype(jnp.bfloat16)
    output = jnp.dot(hidden, down_w, preferred_element_type=jnp.float32)
    fwd_total = scatter((column_f[:, None] * output).astype(jnp.bfloat16))
    out_f = (fwd_x.astype(jnp.float32) + fwd_total).astype(jnp.bfloat16)
    sent_next = from_behind(out_f, "section", 1)

    grad_gate = onto(d_gate, rows_b).astype(jnp.bfloat16)
    grad_up = onto(d_up, rows_b).astype(jnp.bfloat16)
    grad_down = onto(b_hidden, scaled).astype(jnp.bfloat16)
    return (sent_next[None], sent_prev[None], grad_gate[None], grad_up[None], grad_down[None])


def solution(mesh):
    whole = P("section", None, None)
    split = P("section", "expert", None)
    in_specs = (split,) * 6 + (whole,) * 2 + (split,) * 2
    return jax.shard_map(
        local, mesh=mesh, in_specs=in_specs, out_specs=(split,) * 5, check_vma=False
    )
```

```python
import jax
import jax.numpy as jnp
from jax import lax
from jax.sharding import PartitionSpec as P

BLOCK = 128
HSPLIT = 8
NX = 4
NZ = 4
LANES = 128


def shift_x(a, by):
    pairs = [(x * NZ + z, (x + by) % NX * NZ + z) for x in range(NX) for z in range(NZ)]
    return lax.ppermute(a, "expert", pairs)


def shift_z(a, by):
    pairs = [(x * NZ + z, x * NZ + (z + by) % NZ) for x in range(NX) for z in range(NZ)]
    return lax.ppermute(a, "expert", pairs)


def from_behind(x, axis, by):
    length = lax.axis_size(axis)
    pairs = [(i, i + by) for i in range(length) if 0 <= i + by < length]
    return lax.ppermute(x, axis, pairs)


def after(a, *deps):
    return lax.optimization_barrier((a, deps))[0]


def along_z(own):
    return [shift_z(own, k) for k in range(1, NZ)]


def both_ways(a):
    return shift_x(a, 1), shift_x(a, -1)


def joined(*pieces):
    return jnp.concatenate(pieces, axis=0)


def added(*terms):
    total = terms[0].astype(jnp.float32)
    for term in terms[1:]:
        total = total + term.astype(jnp.float32)
    return total


def scatter(parts, *deps):
    half = BLOCK // 2
    low_0, high_0, low_1, high_1, low_2, high_2, low_3, high_3 = [
        parts[i * half:(i + 1) * half] for i in range(8)
    ]
    low_2, high_2 = after((low_2, high_2), *deps)
    low_2 = shift_x(low_2, -1)
    high_2 = shift_x(high_2, 1)
    start = (low_2, high_2)
    back_1 = shift_x(joined(added(low_1, low_2).astype(jnp.bfloat16), high_1), -1)
    back_3 = shift_x(joined(low_3, added(high_3, high_2).astype(jnp.bfloat16)), 1)
    here = added(joined(low_0, high_0), back_1, back_3)
    rows = BLOCK // NZ
    line = [
        shift_z(here[k * rows:(k + 1) * rows].astype(jnp.bfloat16), -k) for k in range(1, NZ)
    ]
    return added(here[:rows], *line), start, (back_1, back_3)


def weights_of(marks, valid, total):
    below = jnp.sum((marks[None, :] <= marks[:, None]).astype(jnp.float32), axis=1)
    gates = ((1.0 + below) / (1.0 + total)).astype(jnp.bfloat16)
    return gates.astype(jnp.float32) * jnp.repeat(valid, BLOCK)


def chosen(blocks, x):
    order = lax.rem(x - jnp.arange(NX, dtype=jnp.int32) + NX, NX)
    return jnp.any(blocks[None, :] == order[:, None], axis=1).astype(jnp.float32)


def across(a, b):
    return lax.dot_general(a, b, (((1,), (1,)), ((), ())), preferred_element_type=jnp.float32)


def onto(a, b):
    return lax.dot_general(a, b, (((0,), (0,)), ((), ())), preferred_element_type=jnp.float32)


def local(
    fwd_tokens,
    bwd_tokens,
    out_grads,
    w_gate,
    w_up,
    w_down,
    fwd_blocks,
    bwd_blocks,
    fwd_buckets,
    bwd_buckets,
):
    place = lax.axis_index("expert")
    group = place // HSPLIT
    x = place // NZ
    total = fwd_tokens.shape[1] * lax.axis_size("expert")
    fwd_x = fwd_tokens[0]
    bwd_x = bwd_tokens[0]
    cotan = out_grads[0]
    both_w = joined(w_gate[0], w_up[0])
    down_w = w_down[0]
    hidden_units = down_w.shape[0]
    valid_f = chosen(lax.dynamic_index_in_dim(fwd_blocks[0], group, 0, keepdims=False), x)
    valid_b = chosen(lax.dynamic_index_in_dim(bwd_blocks[0], group, 0, keepdims=False), x)

    n, width = bwd_x.shape
    marks = jnp.concatenate([fwd_buckets[0], bwd_buckets[0]], axis=1).astype(jnp.bfloat16)
    tagged = jnp.pad(marks, ((0, 0), (0, LANES - marks.shape[1])))
    tagged = jnp.concatenate([bwd_x, tagged], axis=1)
    line_dy = along_z(cotan)
    packed = joined(jnp.pad(joined(cotan, fwd_x), ((0, 0), (0, LANES))), tagged)
    own_1, own_3 = both_ways(packed)
    line_b = along_z(after(tagged, own_1, own_3, *line_dy))
    rest_b, rest_dy = joined(*line_b), joined(*line_dy)

    def onward(index, one, three):
        own = own_1[index * n:(index + 1) * n, :one.shape[1]]
        return joined(own, one[:n]), three[n:]

    def opposite(low, high):
        return shift_x(low, 1), shift_x(high, -1)

    def whole(index, own, rest, step, last):
        part = slice(index * n, (index + 1) * n)
        left, right = own_1[part, :own.shape[1]], own_3[part, :own.shape[1]]
        return [own, rest, left, step[0], *last, right, step[1]]

    first_dy = both_ways(after(rest_dy, own_1, own_3))
    last_dy = opposite(*onward(0, *first_dy))
    line_f = [shift_z(after(fwd_x, *line_b), 1)]
    line_f.append(shift_z(after(fwd_x, line_f[0]), 2))
    line_f.append(shift_z(after(fwd_x, line_f[1]), 3))
    rest_f = joined(*line_f)
    first_b = both_ways(after(rest_b, *first_dy))
    last_b = opposite(*after(onward(2, *first_b), *last_dy))
    first_f = both_ways(after(rest_f, *last_dy, *first_b))
    last_f = opposite(*after(onward(1, *first_f), *last_b))

    pieces = whole(2, tagged, rest_b, first_b, last_b)
    rows_b = joined(*[a[:, :width] for a in pieces])
    marks = joined(*[a[:, width:] for a in pieces])[:, :4].T.astype(jnp.int32)
    rows_dy = joined(*whole(0, cotan, rest_dy, first_dy, last_dy))
    own_marks = lax.dynamic_slice_in_dim(marks.reshape(2, 2, total), group, 1, 1)
    column_f = weights_of(own_marks[0, 0], valid_f, total)
    column_b = weights_of(own_marks[1, 0], valid_b, total)

    b_both = across(rows_b, both_w)
    b_gate, b_up = b_both[:, :hidden_units], b_both[:, hidden_units:]
    scaled = (column_b[:, None] * rows_dy.astype(jnp.float32)).astype(jnp.bfloat16)
    d_hidden = across(scaled, down_w)
    sig = jax.nn.sigmoid(b_gate)
    active = b_gate * sig
    d_gate = (d_hidden * b_up * sig * (1.0 + b_gate * (1.0 - sig))).astype(jnp.bfloat16)
    d_up = (d_hidden * active).astype(jnp.bfloat16)
    b_hidden = (active * b_up).astype(jnp.bfloat16)
    d_both, b_hidden = lax.optimization_barrier((jnp.concatenate([d_gate, d_up], axis=1), b_hidden))
    back = jnp.dot(d_both, both_w, preferred_element_type=jnp.float32)
    bwd_total, start_b, middle_b = scatter(back.astype(jnp.bfloat16))
    d_in = (cotan.astype(jnp.float32) + bwd_total).astype(jnp.bfloat16)
    sent_prev = from_behind(d_in, "section", -1)

    rows_f = joined(*whole(1, fwd_x, rest_f, first_f, after(last_f, *start_b)))
    pre = across(rows_f, both_w)
    pre_gate, pre_up = pre[:, :hidden_units], pre[:, hidden_units:]
    hidden = (pre_gate * jax.nn.sigmoid(pre_gate) * pre_up).astype(jnp.bfloat16)
    hidden = lax.optimization_barrier(hidden)
    output = jnp.dot(hidden, down_w, preferred_element_type=jnp.float32)
    fwd_total, start_f, _ = scatter(
        (column_f[:, None] * output).astype(jnp.bfloat16), *middle_b
    )
    out_f = (fwd_x.astype(jnp.float32) + fwd_total).astype(jnp.bfloat16)
    sent_next = from_behind(out_f, "section", 1)

    d_both, b_hidden = after((d_both, b_hidden), *start_f)
    grad_gate = onto(d_both[:, :hidden_units], rows_b).astype(jnp.bfloat16)
    grad_up = onto(d_both[:, hidden_units:], rows_b).astype(jnp.bfloat16)
    grad_down = onto(b_hidden, scaled).astype(jnp.bfloat16)
    return (sent_next[None], sent_prev[None], grad_gate[None], grad_up[None], grad_down[None])


def solution(mesh):
    whole = P("section", None, None)
    split = P("section", "expert", None)
    in_specs = (split,) * 6 + (whole,) * 2 + (split,) * 2
    return jax.shard_map(
        local, mesh=mesh, in_specs=in_specs, out_specs=(split,) * 5, check_vma=False
    )
```

```python
import jax
import jax.numpy as jnp
from jax import lax
from jax.sharding import PartitionSpec as P

BLOCK = 128
HSPLIT = 8
NX = 4
NZ = 4
LANES = 128
NEAR_FIRST = (0, 1, 3, 2)


def shift_x(a, by):
    pairs = [(x * NZ + z, (x + by) % NX * NZ + z) for x in range(NX) for z in range(NZ)]
    return lax.ppermute(a, "expert", pairs)


def shift_z(a, by):
    pairs = [(x * NZ + z, x * NZ + (z + by) % NZ) for x in range(NX) for z in range(NZ)]
    return lax.ppermute(a, "expert", pairs)


def from_behind(x, axis, by):
    length = lax.axis_size(axis)
    pairs = [(i, i + by) for i in range(length) if 0 <= i + by < length]
    return lax.ppermute(x, axis, pairs)


def after(a, *deps):
    return lax.optimization_barrier((a, deps))[0]


def both_ways(a):
    return shift_x(a, 1), shift_x(a, -1)


def joined(*pieces):
    return jnp.concatenate(pieces, axis=0)


def added(*terms):
    total = terms[0].astype(jnp.float32)
    for term in terms[1:]:
        total = total + term.astype(jnp.float32)
    return total


def scatter(parts, *deps):
    half = BLOCK // 2
    low_0, high_0, low_1, high_1, low_3, high_3, low_2, high_2 = [
        parts[i * half:(i + 1) * half] for i in range(8)
    ]
    low_2, high_2 = after((low_2, high_2), *deps)
    low_2 = shift_x(low_2, -1)
    high_2 = shift_x(high_2, 1)
    back_1 = shift_x(joined(added(low_1, low_2).astype(jnp.bfloat16), high_1), -1)
    back_3 = shift_x(joined(low_3, added(high_3, high_2).astype(jnp.bfloat16)), 1)
    here = added(joined(low_0, high_0), back_1, back_3)
    rows = BLOCK // NZ
    line = [
        shift_z(here[i * rows:(i + 1) * rows].astype(jnp.bfloat16), -NEAR_FIRST[i])
        for i in range(1, NZ)
    ]
    return added(here[:rows], *line), (low_2, high_2), (back_1, back_3)


def weights_of(marks, valid, total):
    below = jnp.sum((marks[None, :] <= marks[:, None]).astype(jnp.float32), axis=1)
    gates = ((1.0 + below) / (1.0 + total)).astype(jnp.bfloat16)
    return gates.astype(jnp.float32) * jnp.repeat(valid, BLOCK)


def chosen(blocks, x):
    order = lax.rem(x - jnp.array(NEAR_FIRST, dtype=jnp.int32) + NX, NX)
    return jnp.any(blocks[None, :] == order[:, None], axis=1).astype(jnp.float32)


def across(a, b):
    return lax.dot_general(a, b, (((1,), (1,)), ((), ())), preferred_element_type=jnp.float32)


def onto(a, b):
    return lax.dot_general(a, b, (((0,), (0,)), ((), ())), preferred_element_type=jnp.float32)


def local(
    fwd_tokens,
    bwd_tokens,
    out_grads,
    w_gate,
    w_up,
    w_down,
    fwd_blocks,
    bwd_blocks,
    fwd_buckets,
    bwd_buckets,
):
    place = lax.axis_index("expert")
    group = place // HSPLIT
    x = place // NZ
    total = fwd_tokens.shape[1] * lax.axis_size("expert")
    fwd_x = fwd_tokens[0]
    bwd_x = bwd_tokens[0]
    cotan = out_grads[0]
    both_w = joined(w_gate[0], w_up[0])
    down_w = w_down[0]
    hidden_units = down_w.shape[0]
    valid_f = chosen(lax.dynamic_index_in_dim(fwd_blocks[0], group, 0, keepdims=False), x)
    valid_b = chosen(lax.dynamic_index_in_dim(bwd_blocks[0], group, 0, keepdims=False), x)

    n, width = bwd_x.shape
    marks = jnp.concatenate([fwd_buckets[0], bwd_buckets[0]], axis=1).astype(jnp.bfloat16)
    tags = jnp.pad(marks, ((0, 0), (0, LANES - marks.shape[1])))
    tagged = jnp.concatenate([cotan, tags], axis=1)
    pair = joined(bwd_x, fwd_x)
    own_1, own_3 = both_ways(joined(tagged, jnp.pad(pair, ((0, 0), (0, LANES)))))
    line = [shift_z(tagged, k) for k in NEAR_FIRST[1:]]
    tied = after(pair, own_1, own_3, *line)
    near = [shift_z(tied, k) for k in NEAR_FIRST[1:3]]
    far = shift_z(after(pair, *near), NEAR_FIRST[3])

    line = joined(*line)
    line_1, line_3 = both_ways(after(line, own_1, own_3))
    low = shift_x(joined(own_1[:n], line_1[:n]), 1)
    high = shift_x(line_3[n:], -1)
    pieces = [tagged, line, own_1[:n], line_1, own_3[:n], line_3, low, high]
    rows_dy = joined(*[a[:, :width] for a in pieces])
    marks = joined(*[a[:, width:] for a in pieces])[:, :4].T.astype(jnp.int32)
    own_marks = lax.dynamic_slice_in_dim(marks.reshape(2, 2, total), group, 1, 1)
    column_f = weights_of(own_marks[0, 0], valid_f, total)
    column_b = weights_of(own_marks[1, 0], valid_b, total)

    near = joined(near[0][:n], near[1][:n], near[0][n:], near[1][n:])
    near_1, near_3 = both_ways(after(near, line_1, line_3))
    far_1, far_3 = both_ways(after(far, near_1, near_3))

    def pieces_of(own, index):
        rows = slice((index + 1) * n, (index + 2) * n)
        left, right = own_1[rows, :width], own_3[rows, :width]
        close = slice(2 * index * n, 2 * (index + 1) * n)
        last = slice(index * n, (index + 1) * n)
        first = joined(
            own, near[close], far[last], left, near_1[close], far_1[last], right, near_3[close], far_3[last]
        )
        low = joined(left, near_1[close][:n])
        high = joined(near_3[close][n:], far_3[last])
        return first, shift_x(low, 1), shift_x(high, -1)

    first_b, low_b, high_b = pieces_of(bwd_x, 0)
    first_f, low_f, high_f = pieces_of(fwd_x, 1)

    scaled = (column_b[:, None] * rows_dy.astype(jnp.float32)).astype(jnp.bfloat16)
    d_hidden = lax.optimization_barrier(across(scaled, down_w))
    last_b = joined(low_b, high_b)
    b_both = joined(lax.optimization_barrier(across(first_b, both_w)), across(last_b, both_w))
    b_gate, b_up = b_both[:, :hidden_units], b_both[:, hidden_units:]
    sig = jax.nn.sigmoid(b_gate)
    active = b_gate * sig
    d_gate = (d_hidden * b_up * sig * (1.0 + b_gate * (1.0 - sig))).astype(jnp.bfloat16)
    d_up = (d_hidden * active).astype(jnp.bfloat16)
    b_hidden = (active * b_up).astype(jnp.bfloat16)
    d_both, b_hidden = lax.optimization_barrier((jnp.concatenate([d_gate, d_up], axis=1), b_hidden))
    back = jnp.dot(d_both, both_w, preferred_element_type=jnp.float32)
    bwd_total, start_b, middle_b = scatter(back.astype(jnp.bfloat16))
    d_in = (cotan.astype(jnp.float32) + bwd_total).astype(jnp.bfloat16)
    sent_prev = from_behind(d_in, "section", -1)

    low_f, high_f = after((low_f, high_f), *start_b)
    pre = joined(lax.optimization_barrier(across(first_f, both_w)), across(joined(low_f, high_f), both_w))
    pre_gate, pre_up = pre[:, :hidden_units], pre[:, hidden_units:]
    hidden = (pre_gate * jax.nn.sigmoid(pre_gate) * pre_up).astype(jnp.bfloat16)
    hidden = lax.optimization_barrier(hidden)
    sent_next = []
    deps = middle_b
    for columns in (slice(0, width // 2), slice(width // 2, width)):
        output = jnp.dot(hidden, down_w[:, columns], preferred_element_type=jnp.float32)
        fwd_total, deps, _ = scatter((column_f[:, None] * output).astype(jnp.bfloat16), *deps)
        out_f = (fwd_x[:, columns].astype(jnp.float32) + fwd_total).astype(jnp.bfloat16)
        sent_next.append(from_behind(out_f, "section", 1))
    sent_next = jnp.concatenate(sent_next, axis=1)

    d_both, b_hidden = after((d_both, b_hidden), *deps)
    rows_b = joined(first_b, last_b)
    grad_gate = onto(d_both[:, :hidden_units], rows_b).astype(jnp.bfloat16)
    grad_up = onto(d_both[:, hidden_units:], rows_b).astype(jnp.bfloat16)
    grad_down = onto(b_hidden, scaled).astype(jnp.bfloat16)
    return (sent_next[None], sent_prev[None], grad_gate[None], grad_up[None], grad_down[None])


def solution(mesh):
    whole = P("section", None, None)
    split = P("section", "expert", None)
    in_specs = (split,) * 6 + (whole,) * 2 + (split,) * 2
    return jax.shard_map(
        local, mesh=mesh, in_specs=in_specs, out_specs=(split,) * 5, check_vma=False
    )
```

```python
import jax
import jax.numpy as jnp
from jax import lax
from jax.sharding import PartitionSpec as P

BLOCK = 128
HSPLIT = 8
NX = 4
NZ = 4
LANES = 128
NEAR_FIRST = (0, 1, 3, 2)


def shift_x(a, by):
    pairs = [(x * NZ + z, (x + by) % NX * NZ + z) for x in range(NX) for z in range(NZ)]
    return lax.ppermute(a, "expert", pairs)


def shift_z(a, by):
    pairs = [(x * NZ + z, x * NZ + (z + by) % NZ) for x in range(NX) for z in range(NZ)]
    return lax.ppermute(a, "expert", pairs)


def from_behind(x, axis, by):
    length = lax.axis_size(axis)
    pairs = [(i, i + by) for i in range(length) if 0 <= i + by < length]
    return lax.ppermute(x, axis, pairs)


def after(a, *deps):
    return lax.optimization_barrier((a, deps))[0]


def both_ways(a):
    return shift_x(a, 1), shift_x(a, -1)


def joined(*pieces):
    return jnp.concatenate(pieces, axis=0)


def added(*terms):
    total = terms[0].astype(jnp.float32)
    for term in terms[1:]:
        total = total + term.astype(jnp.float32)
    return total


def scatter(parts, *deps, far_last=False):
    half = BLOCK // 2
    low_0, high_0, low_1, high_1, low_3, high_3, low_2, high_2 = [
        parts[i * half:(i + 1) * half] for i in range(8)
    ]
    low_2, high_2 = sent = after((low_2, high_2), *deps)
    low_2 = shift_x(low_2, -1)
    high_2 = shift_x(high_2, 1)
    back_1 = shift_x(joined(added(low_1, low_2).astype(jnp.bfloat16), high_1), -1)
    back_3 = shift_x(joined(low_3, added(high_3, high_2).astype(jnp.bfloat16)), 1)
    here = added(joined(low_0, high_0), back_1, back_3)
    rows = BLOCK // NZ
    chunks = [here[i * rows:(i + 1) * rows].astype(jnp.bfloat16) for i in range(1, NZ)]
    line = [shift_z(chunk, -k) for chunk, k in zip(chunks[:2], NEAR_FIRST[1:])]
    last = after(chunks[2], *line) if far_last else chunks[2]
    line.append(shift_z(last, -NEAR_FIRST[3]))
    return added(here[:rows], *line), sent, (low_2, high_2), (back_1, back_3)


def weights_of(marks, valid, total):
    below = jnp.sum((marks[None, :] <= marks[:, None]).astype(jnp.float32), axis=1)
    gates = ((1.0 + below) / (1.0 + total)).astype(jnp.bfloat16)
    return gates.astype(jnp.float32) * jnp.repeat(valid, BLOCK)


def chosen(blocks, x):
    order = lax.rem(x - jnp.array(NEAR_FIRST, dtype=jnp.int32) + NX, NX)
    return jnp.any(blocks[None, :] == order[:, None], axis=1).astype(jnp.float32)


def across(a, b):
    return lax.dot_general(a, b, (((1,), (1,)), ((), ())), preferred_element_type=jnp.float32)


def onto(a, b):
    return lax.dot_general(a, b, (((0,), (0,)), ((), ())), preferred_element_type=jnp.float32)


def local(
    fwd_tokens,
    bwd_tokens,
    out_grads,
    w_gate,
    w_up,
    w_down,
    fwd_blocks,
    bwd_blocks,
    fwd_buckets,
    bwd_buckets,
):
    place = lax.axis_index("expert")
    group = place // HSPLIT
    x = place // NZ
    total = fwd_tokens.shape[1] * lax.axis_size("expert")
    fwd_x = fwd_tokens[0]
    bwd_x = bwd_tokens[0]
    cotan = out_grads[0]
    both_w = joined(w_gate[0], w_up[0])
    down_w = w_down[0]
    hidden_units = down_w.shape[0]
    valid_f = chosen(lax.dynamic_index_in_dim(fwd_blocks[0], group, 0, keepdims=False), x)
    valid_b = chosen(lax.dynamic_index_in_dim(bwd_blocks[0], group, 0, keepdims=False), x)

    n, width = bwd_x.shape
    marks = jnp.concatenate([fwd_buckets[0], bwd_buckets[0]], axis=1).astype(jnp.bfloat16)
    tags = jnp.pad(marks, ((0, 0), (0, LANES - marks.shape[1])))
    tagged = jnp.concatenate([cotan, tags], axis=1)
    pair = joined(bwd_x, fwd_x)
    own_1, own_3 = both_ways(joined(tagged, jnp.pad(pair, ((0, 0), (0, LANES)))))
    line = [shift_z(tagged, k) for k in NEAR_FIRST[1:]]
    tied = after(pair, own_1, own_3, *line)
    near = [shift_z(tied, k) for k in NEAR_FIRST[1:3]]
    far = shift_z(after(pair, *near), NEAR_FIRST[3])

    line = joined(*line)
    line_1, line_3 = both_ways(line)
    low = shift_x(joined(own_1[:n], line_1[:n]), 1)
    high = shift_x(line_3[n:], -1)
    pieces = [tagged, line, own_1[:n], line_1, own_3[:n], line_3, low, high]
    rows_dy = joined(*[a[:, :width] for a in pieces])
    marks = joined(*[a[:, width:] for a in pieces])[:, :4].T.astype(jnp.int32)
    own_marks = lax.dynamic_slice_in_dim(marks.reshape(2, 2, total), group, 1, 1)
    column_f = weights_of(own_marks[0, 0], valid_f, total)
    column_b = weights_of(own_marks[1, 0], valid_b, total)

    near = joined(near[0][:n], near[1][:n], near[0][n:], near[1][n:])
    near_1, near_3 = both_ways(after(near, line_1, line_3))
    far_1, far_3 = both_ways(far)

    def pieces_of(own, index, *deps):
        rows = slice((index + 1) * n, (index + 2) * n)
        left, right = own_1[rows, :width], own_3[rows, :width]
        close = slice(2 * index * n, 2 * (index + 1) * n)
        last = slice(index * n, (index + 1) * n)
        first = [own, near[close], far[last], left, near_1[close], far_1[last], right, near_3[close], far_3[last]]
        low = joined(left, near_1[close][:n])
        high = joined(near_3[close][n:], far_3[last])
        low, high = after((low, high), *deps)
        return after(first, low, high), shift_x(low, 1), shift_x(high, -1)

    first_b, low_b, high_b = pieces_of(bwd_x, 0)
    first_f, low_f, high_f = pieces_of(fwd_x, 1, low_b, high_b)

    scaled = (column_b[:, None] * rows_dy.astype(jnp.float32)).astype(jnp.bfloat16)
    d_hidden = lax.optimization_barrier(across(scaled, down_w))
    first_b, last_b = joined(*first_b), joined(low_b, high_b)
    b_both = joined(lax.optimization_barrier(across(first_b, both_w)), across(last_b, both_w))
    b_gate, b_up = b_both[:, :hidden_units], b_both[:, hidden_units:]
    sig = jax.nn.sigmoid(b_gate)
    active = b_gate * sig
    d_gate = (d_hidden * b_up * sig * (1.0 + b_gate * (1.0 - sig))).astype(jnp.bfloat16)
    d_up = (d_hidden * active).astype(jnp.bfloat16)
    b_hidden = (active * b_up).astype(jnp.bfloat16)
    d_both, b_hidden = lax.optimization_barrier((jnp.concatenate([d_gate, d_up], axis=1), b_hidden))
    back = jnp.dot(d_both, both_w, preferred_element_type=jnp.float32)
    bwd_total, sent_b, start_b, middle_b = scatter(back.astype(jnp.bfloat16), far_last=True)
    d_in = (cotan.astype(jnp.float32) + bwd_total).astype(jnp.bfloat16)
    sent_prev = from_behind(d_in, "section", -1)

    low_f, high_f = after((low_f, high_f), *start_b)
    first_f = joined(*after(first_f, *sent_b))
    pre = joined(lax.optimization_barrier(across(first_f, both_w)), across(joined(low_f, high_f), both_w))
    pre_gate, pre_up = pre[:, :hidden_units], pre[:, hidden_units:]
    hidden = (pre_gate * jax.nn.sigmoid(pre_gate) * pre_up).astype(jnp.bfloat16)
    hidden = lax.optimization_barrier(hidden)
    sent_next = []
    deps = middle_b
    for columns in (slice(0, width // 2), slice(width // 2, width)):
        output = jnp.dot(hidden, down_w[:, columns], preferred_element_type=jnp.float32)
        fwd_total, _, deps, _ = scatter((column_f[:, None] * output).astype(jnp.bfloat16), *deps)
        out_f = (fwd_x[:, columns].astype(jnp.float32) + fwd_total).astype(jnp.bfloat16)
        sent_next.append(from_behind(out_f, "section", 1))
    sent_next = jnp.concatenate(sent_next, axis=1)

    d_both, b_hidden = after((d_both, b_hidden), *deps)
    rows_b = joined(first_b, last_b)
    grad_gate = onto(d_both[:, :hidden_units], rows_b).astype(jnp.bfloat16)
    grad_up = onto(d_both[:, hidden_units:], rows_b).astype(jnp.bfloat16)
    grad_down = onto(b_hidden, scaled).astype(jnp.bfloat16)
    return (sent_next[None], sent_prev[None], grad_gate[None], grad_up[None], grad_down[None])


def solution(mesh):
    whole = P("section", None, None)
    split = P("section", "expert", None)
    in_specs = (split,) * 6 + (whole,) * 2 + (split,) * 2
    return jax.shard_map(
        local, mesh=mesh, in_specs=in_specs, out_specs=(split,) * 5, check_vma=False
    )
```
